32 devices in a mesh: shard: 8 (over z, y), ctx: 2 (over x), dp: 2 (over core).
Axes of the slice: x: 2, y: 2, z: 4, core: 2. Of those that a mesh axis runs over, the one named last changes fastest.
Arguments:
- tokens: bfloat16 [16, 2048, 960], P(('shard', 'dp'), 'ctx'), may hold values from -6 to 6
- attn_gain: bfloat16 [960], P('shard'), may hold values from 0.5 to 1.5
- w_query: bfloat16 [960, 960], P('shard'), may hold values from -0.1875 to 0.1875
- w_key: bfloat16 [960, 320], P('shard'), may hold values from -0.1875 to 0.1875
- w_value: bfloat16 [960, 320], P('shard'), may hold values from -0.1875 to 0.1875
- w_out: bfloat16 [960, 960], P('shard'), may hold values from -1.5 to 1.5
- ffn_gain: bfloat16 [960], P('shard'), may hold values from 0.5 to 1.5
- w_gate: bfloat16 [960, 2560], P('shard'), may hold values from -0.1875 to 0.1875
- w_up: bfloat16 [960, 2560], P('shard'), may hold values from -0.1875 to 0.1875
- w_down: bfloat16 [2560, 960], P('shard'), may hold values from -0.125 to 0.125
- out_grad: bfloat16 [16, 2048, 960], P(('shard', 'dp'), 'ctx'), may hold values from -6 to 6
- piece_order: int32 [8], replicated, may hold values from 0 to 7, as said below
Outputs:
- output: bfloat16 [16, 2048, 960], P(('shard', 'dp'), 'ctx')
- input_grad: bfloat16 [16, 2048, 960], P(('shard', 'dp'), 'ctx')
- grad_attn_gain: float32 [960], P('shard')
- grad_w_query: float32 [960, 960], P('shard')
- grad_w_key: float32 [960, 320], P('shard')
- grad_w_value: float32 [960, 320], P('shard')
- grad_w_out: float32 [960, 960], P('shard')
- grad_ffn_gain: float32 [960], P('shard')
- grad_w_gate: float32 [960, 2560], P('shard')
- grad_w_up: float32 [960, 2560], P('shard')
- grad_w_down: float32 [2560, 960], P('shard')
The draws below stay inside these ranges and needn't reach their ends.
Inputs may be any that keep to these rules, and one draw needn't show every extreme that they name: `piece_order`: entries 4j to 4j + 3 name the four pieces of 256 rows each that the j-th device along ctx holds, in the order of its rows; all entries together are a permutation of 0 to 7, and entries 2i and 2i + 1 sum to 7 for every i.
All inputs are finite; a program needn't handle non-finite values.
Results may differ from the reference program's by a relative error of at most 0.019.
Values may be sent and summed in bfloat16 or wider, within the bound.
A program may use at most 384 MiB of HBM per device.

```python
from functools import partial
import jax
import jax.numpy as jnp
from jax import lax

D = 960
HEADS = 15
KVH = 5
HD = 64
FF = 2560
SEQ_LEN = 2048
BATCH = 16
PIECES = 8
PIECE = 256


def draw_piece_order(key, part):
    key = jax.random.fold_in(key, 7)
    order_key, flip_key = jax.random.split(key)
    pair_count = PIECES // 2
    order = jax.random.permutation(order_key, pair_count).astype(jnp.int32)
    flipped = jax.random.randint(flip_key, (pair_count,), 0, 2, dtype=jnp.int32)
    leading = jnp.where(flipped == 1, PIECES - 1 - order, order).astype(jnp.int32)
    return jnp.stack([leading, PIECES - 1 - leading], axis=1).reshape(PIECES).astype(jnp.int32)


def steps_of(key, extent, pieces, smallest, largest):
    loudness = 1.0
    for axis_at, shards_of in pieces:
        steps = jax.random.uniform(jax.random.fold_in(jax.random.fold_in(key, 6), axis_at), (shards_of,), jnp.float32, smallest / len(pieces), largest / len(pieces))
        loudness = loudness * jnp.repeat(jnp.exp(steps), extent[axis_at] // shards_of).reshape((-1,) + (1,) * (len(extent) - 1 - axis_at))
    return loudness


def bell_draw(own_key, extent, scale, limit, pieces=(), held_as=jnp.bfloat16):
    drawn = scale * jax.random.normal(own_key, extent, jnp.float32)
    if pieces:
        drawn = drawn * steps_of(own_key, extent, pieces, -0.22, 0.18)
    return jnp.clip(drawn, -limit, limit).astype(held_as)


def setup_inputs(seed: int = 0) -> dict:
    streams_of = jax.random.split(jax.random.key(seed), 13)
    return {
        "tokens": bell_draw(streams_of[0], (BATCH, SEQ_LEN, D), 1.0, 6.0, ((0, 16), (1, 2))),
        "attn_gain": jnp.clip(1.0 + 0.1 * jax.random.normal(streams_of[1], (D,), jnp.float32), 0.5, 1.5).astype(jnp.bfloat16),
        "w_query": bell_draw(streams_of[2], (D, HEADS * HD), D ** -0.5, 0.1875, ((0, 8),)),
        "w_key": bell_draw(streams_of[3], (D, KVH * HD), D ** -0.5, 0.1875, ((0, 8),)),
        "w_value": bell_draw(streams_of[4], (D, KVH * HD), D ** -0.5, 0.1875, ((0, 8),)),
        "w_out": bell_draw(streams_of[5], (HEADS * HD, D), (D // 64) ** -0.5, 1.5, ((0, 8),)),
        "ffn_gain": jnp.clip(1.0 + 0.1 * jax.random.normal(streams_of[6], (D,), jnp.float32), 0.5, 1.5).astype(jnp.bfloat16),
        "w_gate": bell_draw(streams_of[7], (D, FF), D ** -0.5, 0.1875, ((0, 8),)),
        "w_up": bell_draw(streams_of[8], (D, FF), D ** -0.5, 0.1875, ((0, 8),)),
        "w_down": bell_draw(streams_of[9], (FF, D), FF ** -0.5, 0.125, ((0, 8),)),
        "out_grad": bell_draw(streams_of[10], (BATCH, SEQ_LEN, D), 1.0, 6.0, ((0, 16), (1, 2))),
        "piece_order": draw_piece_order(jax.random.fold_in(streams_of[12], 71), 0),
    }


@jax.custom_vjp
def low(v):
    return lax.optimization_barrier(v.astype(jnp.bfloat16)).astype(jnp.float32)

@jax.custom_vjp
def low_back(v):
    return v

def low_keep(v):
    return (low(v), None)

def low_pass(kept, grad):
    return (grad,)

def back_keep(v):
    return (v, None)

def back_low(kept, grad):
    return (low(grad),)
low.defvjp(low_keep, low_pass)
low_back.defvjp(back_keep, back_low)
EPSILON = 1e-05
ROPE_BASE = 100000.0
NEGATIVE = -1e+30

def product(left, right):
    return jnp.dot(left, right, precision=lax.Precision.HIGHEST, preferred_element_type=jnp.float32)

def rope_tables(positions):
    halfwidth = HD // 2
    inverse = ROPE_BASE ** (-jnp.arange(halfwidth, dtype=jnp.float32) * 2.0 / HD)
    angles = positions.astype(jnp.float32)[:, None] * inverse[None, :]
    return (jnp.cos(angles)[:, None, :], jnp.sin(angles)[:, None, :])

def rotate(vectors, cosine_table, sine_table):
    halfwidth = vectors.shape[-1] // 2
    first_half = vectors[..., :halfwidth]
    second_half = vectors[..., halfwidth:]
    return jnp.concatenate([first_half * cosine_table - second_half * sine_table, second_half * cosine_table + first_half * sine_table], axis=-1)

def rms_norm(values, gain_values):
    inverse = lax.rsqrt(lax.optimization_barrier(jnp.mean(values * values, axis=-1, keepdims=True)) + EPSILON)
    return values * inverse * gain_values

def head_attention(allowed, operands):
    queries, key_rows, value_rows = operands
    scores = jnp.einsum('gqd,kd->gqk', queries, key_rows, precision=lax.Precision.HIGHEST) * float(HD) ** (-0.5)
    scores = low_back(scores)
    scores = jnp.where(allowed[None], scores, NEGATIVE)
    maximum = lax.optimization_barrier(jnp.max(scores, axis=-1, keepdims=True))
    weights = jnp.exp(scores - maximum)
    probabilities = low(weights / lax.optimization_barrier(jnp.sum(weights, axis=-1, keepdims=True)))
    return jnp.einsum('gqk,kd->gqd', probabilities, value_rows, precision=lax.Precision.HIGHEST)

def block_forward(tokens, parameters, positions):
    attn_gain, w_query, w_key, w_value, w_out, ffn_gain, w_gate, w_up, w_down = parameters
    length = tokens.shape[0]
    group_size = HEADS // KVH
    cosine_table, sine_table = rope_tables(positions)
    allowed = positions[None, :] <= positions[:, None]
    normed = low(rms_norm(tokens, attn_gain))
    queries = low(rotate(low_back(product(normed, w_query)).reshape(length, HEADS, HD), cosine_table, sine_table))
    key_rows = low(rotate(low_back(product(normed, w_key)).reshape(length, KVH, HD), cosine_table, sine_table))
    value_rows = low(low_back(product(normed, w_value))).reshape(length, KVH, HD)
    grouped = queries.reshape(length, KVH, group_size, HD).transpose(1, 2, 0, 3)
    attention_out = lax.map(jax.checkpoint(partial(head_attention, allowed)), (grouped, key_rows.transpose(1, 0, 2), value_rows.transpose(1, 0, 2)))
    attended = low(low_back(attention_out.transpose(2, 0, 1, 3).reshape(length, HEADS * HD)))
    hidden = tokens + low_back(product(attended, w_out))
    normed_ffn = low(rms_norm(hidden, ffn_gain))
    gate_lin = low_back(product(normed_ffn, w_gate))
    upward = low_back(product(normed_ffn, w_up))
    activated = low(jax.nn.silu(gate_lin) * upward)
    return hidden + product(activated, w_down)

def reference(tokens, attn_gain, w_query, w_key, w_value, w_out, ffn_gain, w_gate, w_up, w_down, out_grad, piece_order):
    row_index = jnp.arange(SEQ_LEN, dtype=jnp.int32)
    positions = (piece_order[row_index // PIECE] * PIECE + row_index % PIECE).astype(jnp.int32)
    weights = tuple((operand.astype(jnp.float32) for operand in (attn_gain, w_query, w_key, w_value, w_out, ffn_gain, w_gate, w_up, w_down)))

    def forward(values, parameters):
        return block_forward(values, parameters, positions)

    def one_sequence(running, operands):
        sequence, cotangent = operands
        result, pullback = jax.vjp(forward, sequence.astype(jnp.float32), weights)
        sequence_grad, parameter_grads = pullback(cotangent.astype(jnp.float32))
        running = tuple((prior + summand for prior, summand in zip(running, parameter_grads)))
        return (running, (result.astype(jnp.bfloat16), sequence_grad.astype(jnp.bfloat16)))
    initial = tuple((jnp.zeros_like(operand) for operand in weights))
    running, (output, input_grad) = lax.scan(one_sequence, initial, (tokens, out_grad))
    return (output, input_grad, running[0], running[1], running[2], running[3], running[4], running[5], running[6], running[7], running[8])
```

```python
import jax
import jax.numpy as jnp
from jax import lax
from jax.experimental import pallas as pl
from jax.experimental.pallas import tpu as pltpu
from jax.sharding import PartitionSpec as P

HEADS = 15
KVH = 5
GROUP = HEADS // KVH
HD = 64
HALF = HD // 2
LOCAL_PIECES = 4

EPSILON = 1e-05
ROPE_BASE = 100000.0
NEGATIVE = -1e30
LOG2E = 1.4426950408889634
SCALE = HD**-0.5

F32 = jnp.float32
BF16 = jnp.bfloat16


def dot(left, right, left_dim, right_dim):
    return lax.dot_general(
        left, right, (((left_dim,), (right_dim,)), ((), ())), preferred_element_type=F32
    )


def rope_tables(positions):
    inverse = ROPE_BASE ** (-jnp.arange(HALF, dtype=F32) * 2.0 / HD)
    angles = inverse[:, None] * positions.astype(F32)[None, :]
    return (jnp.cos(angles), jnp.sin(angles))


def rotate(vectors, cosine, sine):
    first, second = vectors[..., :HALF, :], vectors[..., HALF:, :]
    return jnp.concatenate(
        (first * cosine - second * sine, second * cosine + first * sine), axis=-2
    )


def causal(rows):
    key_row = lax.broadcasted_iota(jnp.int32, (rows, rows), 0)
    query_row = lax.broadcasted_iota(jnp.int32, (rows, rows), 1)
    return key_row <= query_row


def piece_at(slot, rows):
    return slot // LOCAL_PIECES, pl.ds(pl.multiple_of(lax.rem(slot, LOCAL_PIECES) * rows, rows), rows)


def attend_kernel(mine_ref, slot_ref, q_ref, k_ref, v_ref, o_ref, lse_ref):
    rows = q_ref.shape[-1]
    own = mine_ref[pl.program_id(2)]

    def scores(slot, g):
        holder, span = piece_at(slot, rows)
        keys = k_ref[holder, 0, 0, :, span].T
        return dot(keys, q_ref[0, 0, g], 1, 0) * LOG2E

    def weighted(slot, weights):
        holder, span = piece_at(slot, rows)
        return dot(v_ref[holder, 0, 0, :, span], weights.astype(BF16), 1, 0)

    diagonal = slot_ref[own]
    allowed = causal(rows)
    state = []
    for g in range(GROUP):
        s = jnp.where(allowed, scores(diagonal, g), NEGATIVE)
        top = jnp.max(s, axis=0, keepdims=True)
        w = jnp.exp2(s - top)
        state.append((top, jnp.sum(w, axis=0, keepdims=True), weighted(diagonal, w)))

    def step(p, state):
        slot = slot_ref[p]
        later = []
        for g in range(GROUP):
            top, total, out = state[g]
            s = scores(slot, g)
            new_top = jnp.maximum(top, jnp.max(s, axis=0, keepdims=True))
            w = jnp.exp2(s - new_top)
            shrink = jnp.exp2(top - new_top)
            later.append(
                (
                    new_top,
                    total * shrink + jnp.sum(w, axis=0, keepdims=True),
                    out * shrink + weighted(slot, w),
                )
            )
        return tuple(later)

    state = lax.fori_loop(0, own, step, tuple(state))
    for g in range(GROUP):
        top, total, out = state[g]
        o_ref[0, 0, g] = (out / total).astype(BF16)
        lse_ref[0, 0, pl.ds(g, 1), :] = top + jnp.log2(total)


def attend_back_kernel(
    mine_ref, slot_ref, q_ref, do_ref, o_ref, lse_ref, k_ref, v_ref, dq_ref, dkv_ref, dk_acc, dv_acc
):
    rows = q_ref.shape[-1]
    piece = pl.program_id(2)
    own = mine_ref[piece]

    @pl.when(piece == 0)
    def _():
        dk_acc[...] = jnp.zeros_like(dk_acc)
        dv_acc[...] = jnp.zeros_like(dv_acc)

    deltas = [
        jnp.sum(do_ref[0, 0, g].astype(F32) * o_ref[0, 0, g].astype(F32), axis=0, keepdims=True)
        for g in range(GROUP)
    ]

    def block(slot, masked, dqs):
        holder, span = piece_at(slot, rows)
        keys_t = k_ref[holder, 0, 0, :, span]
        keys = keys_t.T
        values = v_ref[holder, 0, 0, :, span].T
        later = []
        dk = jnp.zeros((rows, HD), F32)
        dv = jnp.zeros((rows, HD), F32)
        for g in range(GROUP):
            s = dot(keys, q_ref[0, 0, g], 1, 0) * LOG2E
            p = jnp.exp2(s - lse_ref[0, 0, pl.ds(g, 1), :])
            if masked:
                p = jnp.where(causal(rows), p, 0.0)
            dp = dot(values, do_ref[0, 0, g], 1, 0)
            ds = (p * (dp - deltas[g])).astype(BF16)
            dv += dot(p.astype(BF16), do_ref[0, 0, g], 1, 1)
            dk += dot(ds, q_ref[0, 0, g], 1, 1)
            dq = dot(keys_t, ds, 1, 0)
            later.append(dq if dqs is None else dqs[g] + dq)
        at = pl.ds(pl.multiple_of(slot * rows, rows), rows)
        dk_acc[at, :] += dk
        dv_acc[at, :] += dv
        return tuple(later)

    dqs = block(slot_ref[own], True, None)
    dqs = lax.fori_loop(0, own, lambda p, dqs: block(slot_ref[p], False, dqs), dqs)
    for g in range(GROUP):
        dq_ref[0, 0, g] = dqs[g] * SCALE

    @pl.when(piece == LOCAL_PIECES - 1)
    def _():
        holders, width = dkv_ref.shape[0], dkv_ref.shape[-1]
        for j in range(holders):
            dkv_ref[j, 0, 0, 0] = dk_acc[pl.ds(j * width, width), :].T.astype(BF16)
            dkv_ref[j, 0, 0, 1] = dv_acc[pl.ds(j * width, width), :].T.astype(BF16)


def attention_specs(holders, width, rows):
    query = pl.BlockSpec((1, 1, GROUP, HD, rows), lambda s, h, i, *_: (s, h, 0, 0, i))
    stat = pl.BlockSpec((1, 1, GROUP, rows), lambda s, h, i, *_: (s, h, 0, i))
    key = pl.BlockSpec((holders, 1, 1, HD, width), lambda s, h, i, *_: (0, s, h, 0, 0))
    value = pl.BlockSpec((holders, 1, 1, HD, width), lambda s, h, i, *_: (0, s, KVH + h, 0, 0))
    return query, stat, key, value


def cost(q, kv, dots):
    seqs, width, seq_len = q.shape[0], q.shape[-1], kv.shape[0] * kv.shape[-1]
    pairs = seqs * HEADS * width * seq_len * 9 // 16
    return pl.CostEstimate(
        flops=pairs * HD * 2 * dots * 2,
        bytes_accessed=q.size * 8 + kv.size * 4,
        transcendentals=pairs,
    )


def attend(mine, slots, q, kv):
    seqs, _, _, _, width = q.shape
    rows = width // LOCAL_PIECES
    query, stat, key, value = attention_specs(kv.shape[0], width, rows)
    return pl.pallas_call(
        attend_kernel,
        grid_spec=pltpu.PrefetchScalarGridSpec(
            num_scalar_prefetch=2,
            grid=(seqs, KVH, LOCAL_PIECES),
            in_specs=[query, key, value],
            out_specs=[query, stat],
        ),
        out_shape=[
            jax.ShapeDtypeStruct(q.shape, BF16),
            jax.ShapeDtypeStruct((seqs, KVH, GROUP, width), F32),
        ],
        compiler_params=pltpu.CompilerParams(vmem_limit_bytes=40 * 1024 * 1024),
        cost_estimate=cost(q, kv, 2),
        name="attend",
    )(mine, slots, q, kv, kv)


def attend_back(mine, slots, q, d_out, out, lse, kv):
    seqs, _, _, _, width = q.shape
    holders = kv.shape[0]
    rows = width // LOCAL_PIECES
    query, stat, key, value = attention_specs(holders, width, rows)
    return pl.pallas_call(
        attend_back_kernel,
        grid_spec=pltpu.PrefetchScalarGridSpec(
            num_scalar_prefetch=2,
            grid=(seqs, KVH, LOCAL_PIECES),
            in_specs=[query, query, query, stat, key, value],
            out_specs=[
                query,
                pl.BlockSpec(
                    (holders, 1, 1, 2, HD, width), lambda s, h, i, *_: (0, s, h, 0, 0, 0)
                ),
            ],
            scratch_shapes=[
                pltpu.VMEM((holders * width, HD), F32),
                pltpu.VMEM((holders * width, HD), F32),
            ],
        ),
        out_shape=[
            jax.ShapeDtypeStruct(q.shape, F32),
            jax.ShapeDtypeStruct((holders, seqs, KVH, 2, HD, width), BF16),
        ],
        compiler_params=pltpu.CompilerParams(vmem_limit_bytes=40 * 1024 * 1024),
        cost_estimate=cost(q, kv, 5),
        name="attend_back",
    )(mine, slots, q, d_out, out, lse, kv, kv)


def gather(block):
    return lax.all_gather(block, "shard", axis=0, tiled=True)


def reduce_owned(grad):
    owned = lax.psum_scatter(grad.astype(BF16), "shard", scatter_dimension=0, tiled=True)
    return lax.psum(owned, ("ctx", "dp")).astype(F32)


def norm(values):
    inverse = lax.rsqrt(jnp.mean(values * values, axis=-1, keepdims=True) + EPSILON)
    return inverse, values * inverse


def norm_back(d_scaled, normed, inverse):
    return inverse * (d_scaled - normed * jnp.mean(d_scaled * normed, axis=-1, keepdims=True))


def shards(
    tokens,
    attn_gain,
    w_query,
    w_key,
    w_value,
    w_out,
    ffn_gain,
    w_gate,
    w_up,
    w_down,
    out_grad,
    piece_order,
):
    seqs, width, model = tokens.shape
    count = seqs * width
    rows = width // LOCAL_PIECES
    q_width = HEADS * HD
    kv_width = KVH * HD
    ff = w_gate.shape[1]

    gains = gather(jnp.stack((attn_gain, ffn_gain), axis=1).astype(F32))
    w_qkv = gather(jnp.concatenate((w_query, w_key, w_value), axis=1))
    w_o = gather(w_out)
    w_gu = gather(jnp.concatenate((w_gate, w_up), axis=1))
    w_d = gather(w_down)
    gain_one, gain_two = gains[:, 0][None], gains[:, 1][None]

    mine = lax.dynamic_slice_in_dim(
        piece_order, lax.axis_index("ctx") * LOCAL_PIECES, LOCAL_PIECES
    )
    slots = jnp.argsort(piece_order).astype(jnp.int32)
    positions = (mine[:, None] * rows + jnp.arange(rows, dtype=jnp.int32)[None, :]).reshape(width)
    cosine, sine = rope_tables(positions)

    x = tokens.reshape(count, model).astype(F32)
    inverse_one, normed_one = norm(x)
    a = (normed_one * gain_one).astype(BF16)
    lin = dot(w_qkv, a, 0, 1).reshape(HEADS + 2 * KVH, HD, seqs, width).transpose(2, 0, 1, 3)
    q = (rotate(lin[:, :HEADS], cosine, sine) * SCALE).astype(BF16)
    q = q.reshape(seqs, KVH, GROUP, HD, width)
    kv = jnp.concatenate(
        (rotate(lin[:, HEADS : HEADS + KVH], cosine, sine), lin[:, HEADS + KVH :]), axis=1
    ).astype(BF16)
    all_kv = lax.all_gather(kv, "ctx", axis=0)
    att, lse = attend(mine, slots, q, all_kv)
    att_t = att.reshape(seqs, q_width, width).transpose(1, 0, 2).reshape(q_width, count)
    hidden = x + dot(att_t, w_o, 0, 0)
    inverse_two, normed_two = norm(hidden)
    b = (normed_two * gain_two).astype(BF16)
    gate = dot(b, w_gu[:, :ff], 1, 0)
    up = dot(b, w_gu[:, ff:], 1, 0)
    sigmoid = jax.nn.sigmoid(gate)
    silu = gate * sigmoid
    act = (silu * up).astype(BF16)
    output = (hidden + dot(act, w_d, 1, 0)).astype(BF16)

    dy = out_grad.reshape(count, model)
    d_act = dot(dy, w_d, 1, 1)
    grad_down = dot(act, dy, 0, 0)
    d_gate = (d_act * up * sigmoid * (1.0 + gate * (1.0 - sigmoid))).astype(BF16)
    d_up = (d_act * silu).astype(BF16)
    d_gu = jnp.concatenate((d_gate, d_up), axis=1)
    grad_gu = dot(b, d_gu, 0, 0)
    d_b = dot(d_gu, w_gu, 1, 1)
    grad_gain_two = jnp.sum(d_b * normed_two, axis=0)
    d_hidden = dy.astype(F32) + norm_back(d_b * gain_two, normed_two, inverse_two)
    dz = d_hidden.astype(BF16)
    grad_out = dot(att_t, dz, 1, 0)
    d_att = dot(w_o, dz, 1, 1).astype(BF16)
    d_att = d_att.reshape(q_width, seqs, width).transpose(1, 0, 2).reshape(q.shape)
    dq, dkv = attend_back(mine, slots, q, d_att, att, lse, all_kv)
    dkv = lax.psum_scatter(dkv, "ctx", scatter_dimension=0, tiled=False).astype(F32)
    dq = rotate(dq, cosine, -sine).astype(BF16).reshape(seqs, q_width, width)
    dk = rotate(dkv[:, :, 0], cosine, -sine).astype(BF16).reshape(seqs, kv_width, width)
    dv = dkv[:, :, 1].astype(BF16).reshape(seqs, kv_width, width)
    d_lin = jnp.concatenate((dq, dk, dv), axis=1).transpose(1, 0, 2).reshape(-1, count)
    grad_qkv = dot(a, d_lin, 0, 1)
    d_a = dot(d_lin, w_qkv, 0, 1)
    grad_gain_one = jnp.sum(d_a * normed_one, axis=0)
    d_x = d_hidden + norm_back(d_a * gain_one, normed_one, inverse_one)

    own_down = reduce_owned(grad_down)
    own_gu = reduce_owned(grad_gu)
    own_out = reduce_owned(grad_out)
    own_qkv = reduce_owned(grad_qkv)
    own_gains = lax.psum(
        lax.psum_scatter(
            jnp.stack((grad_gain_one, grad_gain_two), axis=1),
            "shard",
            scatter_dimension=0,
            tiled=True,
        ),
        ("ctx", "dp"),
    )
    return (
        output.reshape(tokens.shape),
        d_x.astype(BF16).reshape(tokens.shape),
        own_gains[:, 0],
        own_qkv[:, :q_width],
        own_qkv[:, q_width : q_width + kv_width],
        own_qkv[:, q_width + kv_width :],
        own_out,
        own_gains[:, 1],
        own_gu[:, :ff],
        own_gu[:, ff:],
        own_down,
    )


def solution(mesh):
    rows = P(("shard", "dp"), "ctx", None)
    vector, matrix = P("shard"), P("shard", None)
    weights = (vector, matrix, matrix, matrix, matrix, vector, matrix, matrix, matrix)
    return jax.shard_map(
        shards,
        mesh=mesh,
        in_specs=(rows,) + weights + (rows, P()),
        out_specs=(rows, rows) + weights,
        check_vma=False,
    )
```

```python
import jax
import jax.numpy as jnp
from jax import lax
from jax.experimental import pallas as pl
from jax.experimental.pallas import tpu as pltpu
from jax.sharding import PartitionSpec as P

HEADS = 15
KVH = 5
GROUP = HEADS // KVH
HD = 64
HALF = HD // 2
LOCAL_PIECES = 4

EPSILON = 1e-05
ROPE_BASE = 100000.0
NEGATIVE = -1e30
LOG2E = 1.4426950408889634
SCALE = HD**-0.5

F32 = jnp.float32
BF16 = jnp.bfloat16


def dot(left, right, left_dim, right_dim):
    return lax.dot_general(
        left, right, (((left_dim,), (right_dim,)), ((), ())), preferred_element_type=F32
    )


def rope_tables(positions):
    inverse = ROPE_BASE ** (-jnp.arange(HALF, dtype=F32) * 2.0 / HD)
    angles = inverse[:, None] * positions.astype(F32)[None, :]
    return (jnp.cos(angles), jnp.sin(angles))


def rotate(vectors, cosine, sine):
    first, second = vectors[..., :HALF, :], vectors[..., HALF:, :]
    return jnp.concatenate(
        (first * cosine - second * sine, second * cosine + first * sine), axis=-2
    )


def causal(rows):
    key_row = lax.broadcasted_iota(jnp.int32, (rows, rows), 0)
    query_row = lax.broadcasted_iota(jnp.int32, (rows, rows), 1)
    return key_row <= query_row


def piece_at(slot, rows):
    return slot // LOCAL_PIECES, pl.ds(pl.multiple_of(lax.rem(slot, LOCAL_PIECES) * rows, rows), rows)


def attend_kernel(mine_ref, slot_ref, q_ref, k_ref, v_ref, o_ref, lse_ref):
    rows = q_ref.shape[-1]
    own = mine_ref[pl.program_id(2)]

    def scores(slot, g):
        holder, span = piece_at(slot, rows)
        keys = k_ref[holder, 0, 0, :, span].T
        return dot(keys, q_ref[0, 0, g], 1, 0) * LOG2E

    def weighted(slot, weights):
        holder, span = piece_at(slot, rows)
        return dot(v_ref[holder, 0, 0, :, span], weights.astype(BF16), 1, 0)

    diagonal = slot_ref[own]
    allowed = causal(rows)
    state = []
    for g in range(GROUP):
        s = jnp.where(allowed, scores(diagonal, g), NEGATIVE)
        top = jnp.max(s, axis=0, keepdims=True)
        w = jnp.exp2(s - top)
        state.append((top, jnp.sum(w, axis=0, keepdims=True), weighted(diagonal, w)))

    def step(p, state):
        slot = slot_ref[p]
        later = []
        for g in range(GROUP):
            top, total, out = state[g]
            s = scores(slot, g)
            new_top = jnp.maximum(top, jnp.max(s, axis=0, keepdims=True))
            w = jnp.exp2(s - new_top)
            shrink = jnp.exp2(top - new_top)
            later.append(
                (
                    new_top,
                    total * shrink + jnp.sum(w, axis=0, keepdims=True),
                    out * shrink + weighted(slot, w),
                )
            )
        return tuple(later)

    state = lax.fori_loop(0, own, step, tuple(state))
    for g in range(GROUP):
        top, total, out = state[g]
        o_ref[0, 0, g] = (out / total).astype(BF16)
        lse_ref[0, 0, pl.ds(g, 1), :] = top + jnp.log2(total)


def attend_back_kernel(
    mine_ref, slot_ref, q_ref, do_ref, o_ref, lse_ref, k_ref, v_ref, dq_ref, dkv_ref, dk_acc, dv_acc
):
    rows = q_ref.shape[-1]
    piece = pl.program_id(2)
    own = mine_ref[piece]

    @pl.when(piece == 0)
    def _():
        dk_acc[...] = jnp.zeros_like(dk_acc)
        dv_acc[...] = jnp.zeros_like(dv_acc)

    deltas = [
        jnp.sum(do_ref[0, 0, g].astype(F32) * o_ref[0, 0, g].astype(F32), axis=0, keepdims=True)
        for g in range(GROUP)
    ]

    def block(slot, masked, dqs):
        holder, span = piece_at(slot, rows)
        keys_t = k_ref[holder, 0, 0, :, span]
        keys = keys_t.T
        values = v_ref[holder, 0, 0, :, span].T
        later = []
        dk = jnp.zeros((rows, HD), F32)
        dv = jnp.zeros((rows, HD), F32)
        for g in range(GROUP):
            s = dot(keys, q_ref[0, 0, g], 1, 0) * LOG2E
            p = jnp.exp2(s - lse_ref[0, 0, pl.ds(g, 1), :])
            if masked:
                p = jnp.where(causal(rows), p, 0.0)
            dp = dot(values, do_ref[0, 0, g], 1, 0)
            ds = (p * (dp - deltas[g])).astype(BF16)
            dv += dot(p.astype(BF16), do_ref[0, 0, g], 1, 1)
            dk += dot(ds, q_ref[0, 0, g], 1, 1)
            dq = dot(keys_t, ds, 1, 0)
            later.append(dq if dqs is None else dqs[g] + dq)
        at = pl.ds(pl.multiple_of(slot * rows, rows), rows)
        dk_acc[at, :] += dk
        dv_acc[at, :] += dv
        return tuple(later)

    dqs = block(slot_ref[own], True, None)
    dqs = lax.fori_loop(0, own, lambda p, dqs: block(slot_ref[p], False, dqs), dqs)
    for g in range(GROUP):
        dq_ref[0, 0, g] = dqs[g] * SCALE

    @pl.when(piece == LOCAL_PIECES - 1)
    def _():
        holders, width = dkv_ref.shape[0], dkv_ref.shape[-1]
        for j in range(holders):
            dkv_ref[j, 0, 0, 0] = dk_acc[pl.ds(j * width, width), :].T.astype(BF16)
            dkv_ref[j, 0, 0, 1] = dv_acc[pl.ds(j * width, width), :].T.astype(BF16)


def attention_specs(holders, width, rows):
    query = pl.BlockSpec((1, 1, GROUP, HD, rows), lambda s, h, i, *_: (s, h, 0, 0, i))
    stat = pl.BlockSpec((1, 1, GROUP, rows), lambda s, h, i, *_: (s, h, 0, i))
    key = pl.BlockSpec((holders, 1, 1, HD, width), lambda s, h, i, *_: (0, s, h, 0, 0))
    value = pl.BlockSpec((holders, 1, 1, HD, width), lambda s, h, i, *_: (0, s, KVH + h, 0, 0))
    return query, stat, key, value


def cost(q, kv, dots):
    seqs, width, seq_len = q.shape[0], q.shape[-1], kv.shape[0] * kv.shape[-1]
    pairs = seqs * HEADS * width * seq_len * 9 // 16
    return pl.CostEstimate(
        flops=pairs * HD * 2 * dots * 2,
        bytes_accessed=q.size * 8 + kv.size * 4,
        transcendentals=pairs,
    )


def attend(mine, slots, q, kv):
    seqs, _, _, _, width = q.shape
    rows = width // LOCAL_PIECES
    query, stat, key, value = attention_specs(kv.shape[0], width, rows)
    return pl.pallas_call(
        attend_kernel,
        grid_spec=pltpu.PrefetchScalarGridSpec(
            num_scalar_prefetch=2,
            grid=(seqs, KVH, LOCAL_PIECES),
            in_specs=[query, key, value],
            out_specs=[query, stat],
        ),
        out_shape=[
            jax.ShapeDtypeStruct(q.shape, BF16),
            jax.ShapeDtypeStruct((seqs, KVH, GROUP, width), F32),
        ],
        compiler_params=pltpu.CompilerParams(vmem_limit_bytes=40 * 1024 * 1024),
        cost_estimate=cost(q, kv, 2),
        name="attend",
    )(mine, slots, q, kv, kv)


def attend_back(mine, slots, q, d_out, out, lse, kv):
    seqs, _, _, _, width = q.shape
    holders = kv.shape[0]
    rows = width // LOCAL_PIECES
    query, stat, key, value = attention_specs(holders, width, rows)
    return pl.pallas_call(
        attend_back_kernel,
        grid_spec=pltpu.PrefetchScalarGridSpec(
            num_scalar_prefetch=2,
            grid=(seqs, KVH, LOCAL_PIECES),
            in_specs=[query, query, query, stat, key, value],
            out_specs=[
                query,
                pl.BlockSpec(
                    (holders, 1, 1, 2, HD, width), lambda s, h, i, *_: (0, s, h, 0, 0, 0)
                ),
            ],
            scratch_shapes=[
                pltpu.VMEM((holders * width, HD), F32),
                pltpu.VMEM((holders * width, HD), F32),
            ],
        ),
        out_shape=[
            jax.ShapeDtypeStruct(q.shape, F32),
            jax.ShapeDtypeStruct((holders, seqs, KVH, 2, HD, width), BF16),
        ],
        compiler_params=pltpu.CompilerParams(vmem_limit_bytes=40 * 1024 * 1024),
        cost_estimate=cost(q, kv, 5),
        name="attend_back",
    )(mine, slots, q, d_out, out, lse, kv, kv)


def gather(block):
    parts = lax.axis_size("dp") * lax.axis_size("ctx")
    rows = block.shape[0]
    if rows % parts:
        return lax.all_gather(block, "shard", axis=0, tiled=True)
    part = lax.axis_index("dp") * lax.axis_size("ctx") + lax.axis_index("ctx")
    share = lax.dynamic_slice_in_dim(block, part * (rows // parts), rows // parts)
    return lax.all_gather(share, ("shard", "dp", "ctx"), axis=0, tiled=True)


def swap(block, axis):
    return lax.ppermute(block, axis, [(0, 1), (1, 0)])


def add(left, right):
    return (left.astype(F32) + right.astype(F32)).astype(BF16)


def pair_sums(first, second):
    leads = lax.axis_index("dp") == 0
    mine = jnp.where(leads, first, second)
    return add(mine, swap(jnp.where(leads, second, first), "dp"))


def owned_sums(half):
    owned = lax.psum_scatter(half, "shard", scatter_dimension=0, tiled=True)
    owned = add(owned, swap(owned, "ctx"))
    other = swap(owned, "dp")
    leads = lax.axis_index("dp") == 0
    first, second = jnp.where(leads, owned, other), jnp.where(leads, other, owned)
    return first.astype(F32), second.astype(F32)


def norm(values):
    inverse = lax.rsqrt(jnp.mean(values * values, axis=-1, keepdims=True) + EPSILON)
    return inverse, values * inverse


def norm_back(d_scaled, normed, inverse):
    return inverse * (d_scaled - normed * jnp.mean(d_scaled * normed, axis=-1, keepdims=True))


def shards(
    tokens,
    attn_gain,
    w_query,
    w_key,
    w_value,
    w_out,
    ffn_gain,
    w_gate,
    w_up,
    w_down,
    out_grad,
    piece_order,
):
    seqs, width, model = tokens.shape
    count = seqs * width
    rows = width // LOCAL_PIECES
    q_width = HEADS * HD
    kv_width = KVH * HD
    ff = w_gate.shape[1]

    w_qkv = gather(jnp.concatenate((w_query, w_key, w_value), axis=1))
    gains = lax.all_gather(
        jnp.stack((attn_gain, ffn_gain), axis=1).astype(F32), "shard", axis=0, tiled=True
    )
    w_o = gather(w_out)
    w_gu = gather(jnp.concatenate((w_gate, w_up), axis=1))
    w_d = gather(w_down)
    gain_one, gain_two = gains[:, 0][None], gains[:, 1][None]

    mine = lax.dynamic_slice_in_dim(
        piece_order, lax.axis_index("ctx") * LOCAL_PIECES, LOCAL_PIECES
    )
    slots = jnp.argsort(piece_order).astype(jnp.int32)
    positions = (mine[:, None] * rows + jnp.arange(rows, dtype=jnp.int32)[None, :]).reshape(width)
    cosine, sine = rope_tables(positions)

    x = tokens.reshape(count, model).astype(F32)
    inverse_one, normed_one = norm(x)
    a = (normed_one * gain_one).astype(BF16)
    lin = dot(w_qkv, a, 0, 1).reshape(HEADS + 2 * KVH, HD, seqs, width).transpose(2, 0, 1, 3)
    q = (rotate(lin[:, :HEADS], cosine, sine) * SCALE).astype(BF16)
    q = q.reshape(seqs, KVH, GROUP, HD, width)
    kv = jnp.concatenate(
        (rotate(lin[:, HEADS : HEADS + KVH], cosine, sine), lin[:, HEADS + KVH :]), axis=1
    ).astype(BF16)
    far_kv = swap(kv, "ctx")
    leads = lax.axis_index("ctx") == 0
    all_kv = jnp.stack((jnp.where(leads, kv, far_kv), jnp.where(leads, far_kv, kv)))
    att, lse = attend(mine, slots, q, all_kv)
    att_t = att.reshape(seqs, q_width, width).transpose(1, 0, 2).reshape(q_width, count)
    hidden = x + dot(att_t, w_o, 0, 0)
    inverse_two, normed_two = norm(hidden)
    b = (normed_two * gain_two).astype(BF16)
    gate = dot(b, w_gu[:, :ff], 1, 0)
    up = dot(b, w_gu[:, ff:], 1, 0)
    sigmoid = jax.nn.sigmoid(gate)
    silu = gate * sigmoid
    act = (silu * up).astype(BF16)
    output = (hidden + dot(act, w_d, 1, 0)).astype(BF16)

    dy = out_grad.reshape(count, model)
    d_act = dot(dy, w_d, 1, 1)
    grad_down = dot(act, dy, 0, 0)
    d_gate = (d_act * up * sigmoid * (1.0 + gate * (1.0 - sigmoid))).astype(BF16)
    d_up = (d_act * silu).astype(BF16)
    d_b = dot(d_gate, w_gu[:, :ff], 1, 1) + dot(d_up, w_gu[:, ff:], 1, 1)
    half_gu = pair_sums(dot(b, d_gate, 0, 0).astype(BF16), dot(b, d_up, 0, 0).astype(BF16))
    owned_ff = w_down.shape[0]
    grad_down = grad_down.astype(BF16).reshape(-1, 2, owned_ff // 2, model)
    half_down = pair_sums(grad_down[:, 0], grad_down[:, 1]).reshape(-1, model)
    grad_gain_two = jnp.sum(d_b * normed_two, axis=0)
    d_hidden = dy.astype(F32) + norm_back(d_b * gain_two, normed_two, inverse_two)
    dz = d_hidden.astype(BF16)
    grad_out = dot(att_t, dz, 1, 0)
    d_att = dot(w_o, dz, 1, 1).astype(BF16)
    d_att = d_att.reshape(q_width, seqs, width).transpose(1, 0, 2).reshape(q.shape)
    d_att, half_gu, half_down = lax.optimization_barrier((d_att, half_gu, half_down))
    dq, dkv = attend_back(mine, slots, q, d_att, att, lse, all_kv)
    near, far = jnp.where(leads, dkv[0], dkv[1]), jnp.where(leads, dkv[1], dkv[0])
    dkv = near.astype(F32) + swap(far, "ctx").astype(F32)
    dq = rotate(dq, cosine, -sine).astype(BF16).reshape(seqs, q_width, width)
    dk = rotate(dkv[:, :, 0], cosine, -sine).astype(BF16).reshape(seqs, kv_width, width)
    dv = dkv[:, :, 1].astype(BF16).reshape(seqs, kv_width, width)
    d_lin = jnp.concatenate((dq, dk, dv), axis=1).transpose(1, 0, 2).reshape(-1, count)
    grad_qkv = dot(a, d_lin, 0, 1)
    d_a = dot(d_lin, w_qkv, 0, 1)
    grad_gain_one = jnp.sum(d_a * normed_one, axis=0)
    d_x = d_hidden + norm_back(d_a * gain_one, normed_one, inverse_one)

    first = jnp.concatenate(
        (grad_qkv[:, : q_width + kv_width], grad_gain_one[:, None]), axis=1
    ).astype(BF16)
    second = jnp.concatenate(
        (grad_qkv[:, q_width + kv_width :], grad_out, grad_gain_two[:, None]), axis=1
    ).astype(BF16)
    own_gate, own_up = owned_sums(half_gu)
    own_down = jnp.concatenate(owned_sums(half_down), axis=0)
    own_first, own_second = owned_sums(pair_sums(first, second))
    return (
        output.reshape(tokens.shape),
        d_x.astype(BF16).reshape(tokens.shape),
        own_first[:, -1],
        own_first[:, :q_width],
        own_first[:, q_width:-1],
        own_second[:, :kv_width],
        own_second[:, kv_width:-1],
        own_second[:, -1],
        own_gate,
        own_up,
        own_down,
    )


def solution(mesh):
    rows = P(("shard", "dp"), "ctx", None)
    vector, matrix = P("shard"), P("shard", None)
    weights = (vector, matrix, matrix, matrix, matrix, vector, matrix, matrix, matrix)
    return jax.shard_map(
        shards,
        mesh=mesh,
        in_specs=(rows,) + weights + (rows, P()),
        out_specs=(rows, rows) + weights,
        check_vma=False,
    )
```

```python
import jax
import jax.numpy as jnp
from jax import lax
from jax.experimental import pallas as pl
from jax.experimental.pallas import tpu as pltpu
from jax.sharding import PartitionSpec as P

HEADS = 15
KVH = 5
GROUP = HEADS // KVH
HD = 64
HALF = HD // 2
LOCAL_PIECES = 4

EPSILON = 1e-05
ROPE_BASE = 100000.0
NEGATIVE = -1e30
LOG2E = 1.4426950408889634
SCALE = HD**-0.5

F32 = jnp.float32
BF16 = jnp.bfloat16


def dot(left, right, left_dim, right_dim):
    return lax.dot_general(
        left, right, (((left_dim,), (right_dim,)), ((), ())), preferred_element_type=F32
    )


def rope_tables(positions):
    inverse = ROPE_BASE ** (-jnp.arange(HALF, dtype=F32) * 2.0 / HD)
    angles = inverse[:, None] * positions.astype(F32)[None, :]
    return (jnp.cos(angles), jnp.sin(angles))


def rotate(vectors, cosine, sine):
    first, second = vectors[..., :HALF, :], vectors[..., HALF:, :]
    return jnp.concatenate(
        (first * cosine - second * sine, second * cosine + first * sine), axis=-2
    )


def causal(rows):
    key_row = lax.broadcasted_iota(jnp.int32, (rows, rows), 0)
    query_row = lax.broadcasted_iota(jnp.int32, (rows, rows), 1)
    return key_row <= query_row


def piece_at(slot, rows):
    return slot // LOCAL_PIECES, pl.ds(pl.multiple_of(lax.rem(slot, LOCAL_PIECES) * rows, rows), rows)


def attend_kernel(mine_ref, slot_ref, q_ref, k_ref, v_ref, o_ref, lse_ref):
    rows = q_ref.shape[-1]
    own = mine_ref[pl.program_id(2)]

    def scores(slot, g):
        holder, span = piece_at(slot, rows)
        keys = k_ref[holder, 0, 0, :, span].T
        return dot(keys, q_ref[0, 0, g], 1, 0) * LOG2E

    def weighted(slot, weights):
        holder, span = piece_at(slot, rows)
        return dot(v_ref[holder, 0, 0, :, span], weights.astype(BF16), 1, 0)

    diagonal = slot_ref[own]
    allowed = causal(rows)
    state = []
    for g in range(GROUP):
        s = jnp.where(allowed, scores(diagonal, g), NEGATIVE)
        top = jnp.max(s, axis=0, keepdims=True)
        w = jnp.exp2(s - top)
        state.append((top, jnp.sum(w, axis=0, keepdims=True), weighted(diagonal, w)))

    def step(p, state):
        slot = slot_ref[p]
        later = []
        for g in range(GROUP):
            top, total, out = state[g]
            s = scores(slot, g)
            new_top = jnp.maximum(top, jnp.max(s, axis=0, keepdims=True))
            w = jnp.exp2(s - new_top)
            shrink = jnp.exp2(top - new_top)
            later.append(
                (
                    new_top,
                    total * shrink + jnp.sum(w, axis=0, keepdims=True),
                    out * shrink + weighted(slot, w),
                )
            )
        return tuple(later)

    state = lax.fori_loop(0, own, step, tuple(state))
    for g in range(GROUP):
        top, total, out = state[g]
        o_ref[0, 0, g] = (out / total).astype(BF16)
        lse_ref[0, 0, pl.ds(g, 1), :] = top + jnp.log2(total)


def attend_back_kernel(
    mine_ref, slot_ref, q_ref, do_ref, o_ref, lse_ref, k_ref, v_ref, dq_ref, dkv_ref, dk_acc, dv_acc
):
    rows = q_ref.shape[-1]
    piece = pl.program_id(2)
    own = mine_ref[piece]

    @pl.when(piece == 0)
    def _():
        dk_acc[...] = jnp.zeros_like(dk_acc)
        dv_acc[...] = jnp.zeros_like(dv_acc)

    deltas = [
        jnp.sum(do_ref[0, 0, g].astype(F32) * o_ref[0, 0, g].astype(F32), axis=0, keepdims=True)
        for g in range(GROUP)
    ]

    def block(slot, masked, dqs):
        holder, span = piece_at(slot, rows)
        keys_t = k_ref[holder, 0, 0, :, span]
        keys = keys_t.T
        values = v_ref[holder, 0, 0, :, span].T
        later = []
        dk = jnp.zeros((rows, HD), F32)
        dv = jnp.zeros((rows, HD), F32)
        for g in range(GROUP):
            s = dot(keys, q_ref[0, 0, g], 1, 0) * LOG2E
            p = jnp.exp2(s - lse_ref[0, 0, pl.ds(g, 1), :])
            if masked:
                p = jnp.where(causal(rows), p, 0.0)
            dp = dot(values, do_ref[0, 0, g], 1, 0)
            ds = (p * (dp - deltas[g])).astype(BF16)
            dv += dot(p.astype(BF16), do_ref[0, 0, g], 1, 1)
            dk += dot(ds, q_ref[0, 0, g], 1, 1)
            dq = dot(keys_t, ds, 1, 0)
            later.append(dq if dqs is None else dqs[g] + dq)
        at = pl.ds(pl.multiple_of(slot * rows, rows), rows)
        dk_acc[at, :] += dk
        dv_acc[at, :] += dv
        return tuple(later)

    dqs = block(slot_ref[own], True, None)
    dqs = lax.fori_loop(0, own, lambda p, dqs: block(slot_ref[p], False, dqs), dqs)
    for g in range(GROUP):
        dq_ref[0, 0, g] = dqs[g] * SCALE

    @pl.when(piece == LOCAL_PIECES - 1)
    def _():
        holders, width = dkv_ref.shape[0], dkv_ref.shape[-1]
        for j in range(holders):
            dkv_ref[j, 0, 0, 0] = dk_acc[pl.ds(j * width, width), :].T.astype(BF16)
            dkv_ref[j, 0, 0, 1] = dv_acc[pl.ds(j * width, width), :].T.astype(BF16)


def attention_specs(holders, width, rows):
    query = pl.BlockSpec((1, 1, GROUP, HD, rows), lambda s, h, i, *_: (s, h, 0, 0, i))
    stat = pl.BlockSpec((1, 1, GROUP, rows), lambda s, h, i, *_: (s, h, 0, i))
    key = pl.BlockSpec((holders, 1, 1, HD, width), lambda s, h, i, *_: (0, s, h, 0, 0))
    value = pl.BlockSpec((holders, 1, 1, HD, width), lambda s, h, i, *_: (0, s, KVH + h, 0, 0))
    return query, stat, key, value


def cost(q, kv, dots):
    seqs, width, seq_len = q.shape[0], q.shape[-1], kv.shape[0] * kv.shape[-1]
    pairs = seqs * HEADS * width * seq_len * 9 // 16
    return pl.CostEstimate(
        flops=pairs * HD * 2 * dots * 2,
        bytes_accessed=q.size * 8 + kv.size * 4,
        transcendentals=pairs,
    )


def attend(mine, slots, q, kv):
    seqs, _, _, _, width = q.shape
    rows = width // LOCAL_PIECES
    query, stat, key, value = attention_specs(kv.shape[0], width, rows)
    return pl.pallas_call(
        attend_kernel,
        grid_spec=pltpu.PrefetchScalarGridSpec(
            num_scalar_prefetch=2,
            grid=(seqs, KVH, LOCAL_PIECES),
            in_specs=[query, key, value],
            out_specs=[query, stat],
        ),
        out_shape=[
            jax.ShapeDtypeStruct(q.shape, BF16),
            jax.ShapeDtypeStruct((seqs, KVH, GROUP, width), F32),
        ],
        compiler_params=pltpu.CompilerParams(vmem_limit_bytes=40 * 1024 * 1024),
        cost_estimate=cost(q, kv, 2),
        name="attend",
    )(mine, slots, q, kv, kv)


def attend_back(mine, slots, q, d_out, out, lse, kv):
    seqs, _, _, _, width = q.shape
    holders = kv.shape[0]
    rows = width // LOCAL_PIECES
    query, stat, key, value = attention_specs(holders, width, rows)
    return pl.pallas_call(
        attend_back_kernel,
        grid_spec=pltpu.PrefetchScalarGridSpec(
            num_scalar_prefetch=2,
            grid=(seqs, KVH, LOCAL_PIECES),
            in_specs=[query, query, query, stat, key, value],
            out_specs=[
                query,
                pl.BlockSpec(
                    (holders, 1, 1, 2, HD, width), lambda s, h, i, *_: (0, s, h, 0, 0, 0)
                ),
            ],
            scratch_shapes=[
                pltpu.VMEM((holders * width, HD), F32),
                pltpu.VMEM((holders * width, HD), F32),
            ],
        ),
        out_shape=[
            jax.ShapeDtypeStruct(q.shape, F32),
            jax.ShapeDtypeStruct((holders, seqs, KVH, 2, HD, width), BF16),
        ],
        compiler_params=pltpu.CompilerParams(vmem_limit_bytes=40 * 1024 * 1024),
        cost_estimate=cost(q, kv, 5),
        name="attend_back",
    )(mine, slots, q, d_out, out, lse, kv, kv)


def gather(block):
    parts = lax.axis_size("dp") * lax.axis_size("ctx")
    rows = block.shape[0]
    if rows % parts:
        return lax.all_gather(block, "shard", axis=0, tiled=True)
    part = lax.axis_index("dp") * lax.axis_size("ctx") + lax.axis_index("ctx")
    share = lax.dynamic_slice_in_dim(block, part * (rows // parts), rows // parts)
    return lax.all_gather(share, ("shard", "dp", "ctx"), axis=0, tiled=True)


def swap(block, axis):
    return lax.ppermute(block, axis, [(0, 1), (1, 0)])


def add(left, right):
    return (left.astype(F32) + right.astype(F32)).astype(BF16)


def pair_sums(first, second):
    leads = lax.axis_index("dp") == 0
    mine = jnp.where(leads, first, second)
    return add(mine, swap(jnp.where(leads, second, first), "dp"))


def scatter(half):
    return lax.psum_scatter(half, "shard", scatter_dimension=0, tiled=True)


def owned_sums(owned):
    owned = add(owned, swap(owned, "ctx"))
    other = swap(owned, "dp")
    leads = lax.axis_index("dp") == 0
    first, second = jnp.where(leads, owned, other), jnp.where(leads, other, owned)
    return first.astype(F32), second.astype(F32)


def norm(values):
    inverse = lax.rsqrt(jnp.mean(values * values, axis=-1, keepdims=True) + EPSILON)
    return inverse, values * inverse


def norm_back(d_scaled, normed, inverse):
    return inverse * (d_scaled - normed * jnp.mean(d_scaled * normed, axis=-1, keepdims=True))


def shards(
    tokens,
    attn_gain,
    w_query,
    w_key,
    w_value,
    w_out,
    ffn_gain,
    w_gate,
    w_up,
    w_down,
    out_grad,
    piece_order,
):
    seqs, width, model = tokens.shape
    count = seqs * width
    rows = width // LOCAL_PIECES
    q_width = HEADS * HD
    kv_width = KVH * HD
    ff = w_gate.shape[1]

    w_qkv = gather(jnp.concatenate((w_query, w_key, w_value), axis=1))
    gains = lax.all_gather(
        jnp.stack((attn_gain, ffn_gain), axis=1).astype(F32), "shard", axis=0, tiled=True
    )
    w_o = gather(w_out)
    w_gu = gather(jnp.concatenate((w_gate, w_up), axis=1))
    w_d = gather(w_down)
    gain_one, gain_two = gains[:, 0][None], gains[:, 1][None]

    mine = lax.dynamic_slice_in_dim(
        piece_order, lax.axis_index("ctx") * LOCAL_PIECES, LOCAL_PIECES
    )
    slots = jnp.argsort(piece_order).astype(jnp.int32)
    positions = (mine[:, None] * rows + jnp.arange(rows, dtype=jnp.int32)[None, :]).reshape(width)
    cosine, sine = rope_tables(positions)

    x = tokens.reshape(count, model).astype(F32)
    inverse_one, normed_one = norm(x)
    a = (normed_one * gain_one).astype(BF16)
    lin = dot(w_qkv, a, 0, 1).reshape(HEADS + 2 * KVH, HD, seqs, width).transpose(2, 0, 1, 3)
    q = (rotate(lin[:, :HEADS], cosine, sine) * SCALE).astype(BF16)
    q = q.reshape(seqs, KVH, GROUP, HD, width)
    kv = jnp.concatenate(
        (rotate(lin[:, HEADS : HEADS + KVH], cosine, sine), lin[:, HEADS + KVH :]), axis=1
    ).astype(BF16)
    far_kv = swap(kv, "ctx")
    leads = lax.axis_index("ctx") == 0
    all_kv = jnp.stack((jnp.where(leads, kv, far_kv), jnp.where(leads, far_kv, kv)))
    att, lse = attend(mine, slots, q, all_kv)
    att_t = att.reshape(seqs, q_width, width).transpose(1, 0, 2).reshape(q_width, count)
    hidden = x + dot(att_t, w_o, 0, 0)
    inverse_two, normed_two = norm(hidden)
    b = (normed_two * gain_two).astype(BF16)
    gate = dot(b, w_gu[:, :ff], 1, 0)
    up = dot(b, w_gu[:, ff:], 1, 0)
    sigmoid = jax.nn.sigmoid(gate)
    silu = gate * sigmoid
    act = (silu * up).astype(BF16)
    output = (hidden + dot(act, w_d, 1, 0)).astype(BF16)

    dy = out_grad.reshape(count, model)
    d_act = dot(dy, w_d, 1, 1)
    grad_down = dot(act, dy, 0, 0)
    d_gate = (d_act * up * sigmoid * (1.0 + gate * (1.0 - sigmoid))).astype(BF16)
    d_up = (d_act * silu).astype(BF16)
    d_b = dot(d_gate, w_gu[:, :ff], 1, 1) + dot(d_up, w_gu[:, ff:], 1, 1)
    half_gu = pair_sums(dot(b, d_gate, 0, 0).astype(BF16), dot(b, d_up, 0, 0).astype(BF16))
    owned_ff = w_down.shape[0]
    grad_down = grad_down.astype(BF16).reshape(-1, 2, owned_ff // 2, model)
    half_down = pair_sums(grad_down[:, 0], grad_down[:, 1]).reshape(-1, model)
    grad_gain_two = jnp.sum(d_b * normed_two, axis=0)
    d_hidden = dy.astype(F32) + norm_back(d_b * gain_two, normed_two, inverse_two)
    dz = d_hidden.astype(BF16)
    grad_out = dot(att_t, dz, 1, 0)
    d_att = dot(w_o, dz, 1, 1).astype(BF16)
    d_att = d_att.reshape(q_width, seqs, width).transpose(1, 0, 2).reshape(q.shape)
    d_att, half_gu, half_down = lax.optimization_barrier((d_att, half_gu, half_down))
    dq, dkv = attend_back(mine, slots, q, d_att, att, lse, all_kv)
    dq, half_down = lax.optimization_barrier((dq, half_down))
    near, far = jnp.where(leads, dkv[0], dkv[1]), jnp.where(leads, dkv[1], dkv[0])
    dkv = near.astype(F32) + swap(far, "ctx").astype(F32)
    dq = rotate(dq, cosine, -sine).astype(BF16).reshape(seqs, q_width, width)
    dk = rotate(dkv[:, :, 0], cosine, -sine).astype(BF16).reshape(seqs, kv_width, width)
    dv = dkv[:, :, 1].astype(BF16).reshape(seqs, kv_width, width)
    d_lin = jnp.concatenate((dq, dk, dv), axis=1).transpose(1, 0, 2).reshape(-1, count)
    grad_qkv = dot(a, d_lin, 0, 1)
    d_a = dot(d_lin, w_qkv, 0, 1)
    grad_gain_one = jnp.sum(d_a * normed_one, axis=0)
    d_x = d_hidden + norm_back(d_a * gain_one, normed_one, inverse_one)

    first = jnp.concatenate(
        (grad_qkv[:, : q_width + kv_width], grad_gain_one[:, None]), axis=1
    ).astype(BF16)
    second = jnp.concatenate(
        (grad_qkv[:, q_width + kv_width :], grad_out, grad_gain_two[:, None]), axis=1
    ).astype(BF16)
    half_last, part_gu, part_down = lax.optimization_barrier(
        (pair_sums(first, second), scatter(half_gu), scatter(half_down))
    )
    own_first, own_second = owned_sums(scatter(half_last))
    own_gate, own_up = owned_sums(part_gu)
    own_down = jnp.concatenate(owned_sums(part_down), axis=0)
    return (
        output.reshape(tokens.shape),
        d_x.astype(BF16).reshape(tokens.shape),
        own_first[:, -1],
        own_first[:, :q_width],
        own_first[:, q_width:-1],
        own_second[:, :kv_width],
        own_second[:, kv_width:-1],
        own_second[:, -1],
        own_gate,
        own_up,
        own_down,
    )


def solution(mesh):
    rows = P(("shard", "dp"), "ctx", None)
    vector, matrix = P("shard"), P("shard", None)
    weights = (vector, matrix, matrix, matrix, matrix, vector, matrix, matrix, matrix)
    return jax.shard_map(
        shards,
        mesh=mesh,
        in_specs=(rows,) + weights + (rows, P()),
        out_specs=(rows, rows) + weights,
        check_vma=False,
    )
```
